512 devices in a mesh: mem: 32 (over z, x), tp: 16 (over y, core).
Axes of the slice: x: 4, y: 8, z: 8, core: 2. Of those that a mesh axis runs over, the one named last changes fastest.
Arguments:
- tokens: bfloat16 [12288, 2560], P(('mem', 'tp')), may hold values from -48 to 48
- input_weight: bfloat16 [2560, 6144], P(None, 'tp'), may hold values from -0.125 to 0.125
- output_weight: bfloat16 [2048, 2560], P('tp'), may hold values from -0.125 to 0.125
- gate_logit: float32 [16], P('tp'), may hold values from -2 to 2
- memory: bfloat16 [2, 131072, 2048], P(None, 'mem', 'tp'), may hold values from -48 to 48
- retrieved: int32 [96, 16], P('mem'), may hold values from 0 to 1023, as said below
- block_home: int32 [1024], replicated, may hold values from 0 to 1023, as said below
Outputs:
- mixed: bfloat16 [12288, 2560], P(('mem', 'tp'))
The draws below stay inside these ranges and needn't reach their ends.
Inputs may be any that keep to these rules, and one draw needn't show every extreme that they name: `block_home`: A permutation: each logical block names one stored block; stored block s lies with index s // 32 of mem, as its block s % 32. `retrieved`: each row names 16 different logical blocks; rows i * 3 to i * 3 + 2 are the query blocks of index i of mem. A row names at most 2 blocks held by one index of mem, and all rows of one index of mem together name at most 2 different blocks held by one index of mem.
All inputs are finite; a program needn't handle non-finite values.
Results may differ from the reference program's by a relative error of at most 0.023.
Values may be sent and summed in bfloat16 or wider, within the bound.
A program may use at most 128 MiB of HBM per device.

```python
import jax
import jax.numpy as jnp
from jax import lax

D = 2560
HEADS = 16
HD = 128
BLK = 128
TOPB = 16
CAP = 2
MB_DEV = 32
QB_DEV = 3
POOL = 24
TOKENS = 12288
QBLOCKS = 96
MEMBLK = 1024
MEMTOK = 131072
N_TP = 16


def retrieval_tables(key):
    key = jax.random.fold_in(key, 77)
    keys_split = jax.random.split(key, 7)
    holder_count = MEMBLK // MB_DEV
    home = jax.random.permutation(keys_split[0], MEMBLK).astype(jnp.int32)
    block_of_slot = jnp.argsort(home).astype(jnp.int32)
    most_popular = jax.random.randint(keys_split[1], (), 0, holder_count)
    popularity = jax.random.permutation(keys_split[2], holder_count).astype(jnp.int32)
    candidate_blocks = holder_count * CAP
    candidate_holder = jnp.arange(candidate_blocks, dtype=jnp.int32) // CAP
    random_jitter = jax.random.randint(keys_split[3], (holder_count, candidate_blocks), 0, holder_count)
    slight_tilt = (holder_count - popularity[candidate_holder]) // 2
    extra_credit = jnp.where(candidate_holder == most_popular, 4 * holder_count, 0)
    block_ranking = (random_jitter + slight_tilt[None, :] + extra_credit[None, :]) * candidate_blocks + jnp.arange(candidate_blocks, dtype=jnp.int32)[None, :]
    chosen = jnp.argsort(-block_ranking, axis=1)[:, :POOL].astype(jnp.int32)
    pool_owner = chosen // CAP
    pool_member = chosen % CAP
    starting = jax.random.randint(keys_split[4], (holder_count, holder_count), 0, MB_DEV)
    pool_local = (jnp.take_along_axis(starting, pool_owner, axis=1) + pool_member) % MB_DEV
    pool_block = block_of_slot[pool_owner * MB_DEV + pool_local]
    rest = POOL - CAP
    pick_score = jax.random.randint(keys_split[5], (QBLOCKS, rest), 0, 1 << 20) * rest + jnp.arange(rest, dtype=jnp.int32)[None, :]
    picked = jnp.argsort(-pick_score, axis=1)[:, :TOPB - CAP].astype(jnp.int32) + CAP
    leading = jnp.broadcast_to(jnp.arange(CAP, dtype=jnp.int32)[None, :], (QBLOCKS, CAP))
    positions = jnp.concatenate([leading, picked], axis=1)
    order_score = jax.random.randint(keys_split[6], (QBLOCKS, TOPB), 0, 1 << 20) * TOPB + jnp.arange(TOPB, dtype=jnp.int32)[None, :]
    shuffle = jnp.argsort(order_score, axis=1).astype(jnp.int32)
    positions = jnp.take_along_axis(positions, shuffle, axis=1)
    device_of_row = jnp.arange(QBLOCKS, dtype=jnp.int32) // QB_DEV
    lists = jnp.take_along_axis(pool_block[device_of_row], positions, axis=1)
    return (home, lists.astype(jnp.int32))


def draw_retrieved(key, part):
    return retrieval_tables(key)[1]


def draw_block_home(key, part):
    return retrieval_tables(key)[0]


def draw_tokens(key, part):
    values = jnp.clip(jax.random.normal(key, (TOKENS, D), jnp.float32), -6.0, 6.0)
    return values.astype(jnp.bfloat16)


def draw_memory(key, part):
    values = jnp.clip(jax.random.normal(key, (2, MEMTOK, HEADS * HD), jnp.float32), -6.0, 6.0)
    return values.astype(jnp.bfloat16)


def block_scale(key, dims, pieces, low, largest):
    def one(position, parts):
        draws = jax.random.uniform(jax.random.fold_in(jax.random.fold_in(key, 6), position), (parts,), jnp.float32, low / len(pieces), largest / len(pieces))
        return jnp.repeat(jnp.exp(draws), dims[position] // parts).reshape((-1,) + (1,) * (len(dims) - position - 1))

    loudness = one(*pieces[0])
    for cut in pieces[1:]:
        loudness = loudness * one(*cut)
    return loudness


def scatter_about(rng, extent, scale, limit, pieces=(), held_as=jnp.bfloat16):
    level = block_scale(rng, extent, pieces, -0.22, 0.18) if pieces else 1.0
    entries = jax.random.normal(rng, extent, jnp.float32) * scale * level
    return jnp.minimum(jnp.maximum(entries, -limit), limit).astype(held_as)


def setup_inputs(seed: int = 0) -> dict:
    arg_keys = jax.random.split(jax.random.key(seed), 8)
    tokens = draw_tokens(jax.random.fold_in(arg_keys[7], 71), 0)
    input_weight = scatter_about(arg_keys[1], (D, HEADS * 3 * HD), D ** -0.5, 0.125, ((1, 16),))
    output_weight = scatter_about(arg_keys[2], (HEADS * HD, D), (HEADS * HD) ** -0.5, 0.125, ((0, 16),))
    gate_logit = jnp.clip(jax.random.uniform(arg_keys[3], (HEADS,), jnp.float32, -2.0, 2.0) * block_scale(arg_keys[3], (HEADS,), ((0, 16),), -0.4, 0.0), -2.0, 2.0)
    memory = draw_memory(jax.random.fold_in(arg_keys[7], 71), 0)
    retrieved = draw_retrieved(jax.random.fold_in(arg_keys[7], 71), 0)
    block_home = draw_block_home(jax.random.fold_in(arg_keys[7], 71), 0)
    return dict(tokens=tokens, input_weight=input_weight, output_weight=output_weight, gate_logit=gate_logit, memory=memory, retrieved=retrieved, block_home=block_home)


NEG_FILL = -1e30


def softmax_rows(scores, allowed):
    row_peak = jnp.max(jnp.where(allowed, scores, NEG_FILL), axis=-1, keepdims=True)
    weights = jnp.where(allowed, jnp.exp(scores - row_peak), 0.0)
    return (weights / jnp.sum(weights, axis=-1, keepdims=True)).astype(jnp.bfloat16)


def reference(tokens, input_weight, output_weight, gate_logit, memory, retrieved, block_home):
    score_scale = HD ** -0.5
    projected = jnp.dot(tokens, input_weight, preferred_element_type=jnp.float32).astype(jnp.bfloat16)
    projected = projected.reshape(TOKENS, HEADS, 3, HD)
    queries = projected[:, :, 0]
    key_rows = projected[:, :, 1]
    value_rows = projected[:, :, 2]
    zero_rows = jnp.zeros((BLK, HEADS, HD), jnp.bfloat16)
    padded_keys = jnp.concatenate([zero_rows, key_rows], axis=0)
    padded_values = jnp.concatenate([zero_rows, value_rows], axis=0)
    store = memory.reshape(2, MEMBLK, BLK, HEADS, HD)
    mixing = jax.nn.sigmoid(gate_logit)[None, :, None]
    query_index = lax.broadcasted_iota(jnp.int32, (BLK, 2 * BLK), 0)
    key_index = lax.broadcasted_iota(jnp.int32, (BLK, 2 * BLK), 1)

    def one_block(block):
        first_row = (block * BLK).astype(jnp.int32)
        block_queries = lax.dynamic_slice_in_dim(queries, first_row, BLK, 0).astype(jnp.float32)
        near_keys = lax.dynamic_slice_in_dim(padded_keys, first_row, 2 * BLK, 0).astype(jnp.float32)
        near_values = lax.dynamic_slice_in_dim(padded_values, first_row, 2 * BLK, 0).astype(jnp.float32)
        near_scores = jnp.einsum("qhd,khd->hqk", block_queries, near_keys) * score_scale
        allowed = (key_index > query_index) & (key_index <= query_index + BLK) & (key_index + first_row - BLK >= 0)
        near_probs = softmax_rows(near_scores, allowed[None]).astype(jnp.float32)
        near_out = jnp.einsum("hqk,khd->qhd", near_probs, near_values)
        home_slots = jnp.take(block_home, retrieved[block]).astype(jnp.int32)
        far_pairs = jnp.take(store, home_slots, axis=1).reshape(2, TOPB * BLK, HEADS, HD).astype(jnp.float32)
        far_scores = jnp.einsum("qhd,khd->hqk", block_queries, far_pairs[0]) * score_scale
        far_probs = softmax_rows(far_scores, True).astype(jnp.float32)
        far_out = jnp.einsum("hqk,khd->qhd", far_probs, far_pairs[1])
        return (mixing * far_out + (1.0 - mixing) * near_out).astype(jnp.bfloat16)

    attended = lax.map(one_block, jnp.arange(QBLOCKS, dtype=jnp.int32)).reshape(TOKENS, HEADS * HD)
    head_group = HEADS // N_TP
    grouped = attended.reshape(TOKENS, N_TP, head_group * HD)
    weight_groups = output_weight.reshape(N_TP, head_group * HD, D)

    def add_group(total, member):
        term = jnp.dot(grouped[:, member], weight_groups[member], preferred_element_type=jnp.float32)
        rounded = lax.optimization_barrier(term.astype(jnp.bfloat16)).astype(jnp.float32)
        return total + rounded, None

    total, unused = lax.scan(add_group, jnp.zeros((TOKENS, D), jnp.float32), jnp.arange(N_TP, dtype=jnp.int32))
    return total.astype(jnp.bfloat16)
```

```python
import functools

import jax
import jax.numpy as jnp
from jax import lax
from jax.experimental import pallas as pl
from jax.experimental.pallas import tpu as pltpu
from jax.sharding import PartitionSpec as P

HD = 128
BLK = 128
XS = 4
RING = 8
MESH = pl.DeviceIdType.MESH
NONE = -1e30
BF16 = jnp.bfloat16
F32 = jnp.float32


def ring_offset(step):
    half = step // 2
    even = lax.rem(step, 2) == 0 if not isinstance(step, int) else step % 2 == 0
    if isinstance(step, int):
        return (4 - half) if even else (half - 3)
    return jnp.where(even, 4 - half, half - 3)


def kernel(
    tok_ref, rec_ref, gate_ref, wi_hbm, wo_hbm, mem_hbm, out_ref,
    tok_all, x_all, wi_v, wo_v, mem_v,
    flags_v, stage_v, table_v, flags_s, table_s,
    kv_send, kv_all, q_all, keys_v, vals_v, halo,
    near_v, far_v, lse_v, o_send, o_recv, l_send, l_recv,
    part, sib_part, y_send, y_recv,
    in_sem,
    tr_s, tr_r, tl_s, tl_r, ts_s, ts_r,
    fz_s, fz_r, fx_s, fx_r, sm_sem,
    kv_s, kv_r, qr_s, qr_r, ql_s, ql_r, h_s, h_r,
    o_s, o_r, l_s, l_r, ps_s, ps_r, y_s, y_r,
):
    m = lax.axis_index("mem")
    t = lax.axis_index("tp")
    z, x = m // XS, lax.rem(m, XS)
    y, c = t // 2, lax.rem(t, 2)
    sibling = (m, t + 1 - 2 * c)
    y_up = (m, lax.rem(y + 1, RING) * 2 + c)
    y_down = (m, lax.rem(y + RING - 1, RING) * 2 + c)
    z_up = (lax.rem(z + 1, RING) * XS + x, t)
    z_down = (lax.rem(z + RING - 1, RING) * XS + x, t)
    nmem = RING * XS
    following = (lax.rem(m + 1, nmem), t)
    preceding = (lax.rem(m + nmem - 1, nmem), t)

    def x_peer(d):
        return (z * XS + lax.rem(x + d, XS), t)

    def z_peer(d):
        return (lax.rem(z + d, RING) * XS + x, t)

    def send(src, dst, s, r, to):
        return pltpu.make_async_remote_copy(
            src_ref=src, dst_ref=dst, send_sem=s, recv_sem=r, device_id=to, device_id_type=MESH
        )

    loads = [
        pltpu.make_async_copy(mem_hbm, mem_v, in_sem.at[0]),
        pltpu.make_async_copy(wi_hbm, wi_v, in_sem.at[1]),
        pltpu.make_async_copy(wo_hbm, wo_v, in_sem.at[2]),
    ]
    for load in loads:
        load.start()

    barrier = pltpu.get_barrier_semaphore()
    partners = [sibling, y_up, y_down, following, preceding]
    partners += [x_peer(d) for d in range(1, XS)] + [z_peer(d) for d in range(1, RING)]
    for to in partners:
        pl.semaphore_signal(barrier, inc=1, device_id=to, device_id_type=MESH)

    own = tok_ref[...].astype(F32)
    half = own.shape[1] // 2
    rows = own.shape[0]
    tok_all[y, c] = jnp.concatenate([own[:, :half], own[:, half:]], axis=0).astype(BF16)
    flags_v[z] = rec_ref[z]

    pl.semaphore_wait(barrier, len(partners))

    flag_copies = [
        send(rec_ref.at[lax.rem(z + d, RING)], flags_v.at[z], fz_s.at[d - 1], fz_r.at[d - 1], z_peer(d))
        for d in range(1, RING)
    ]

    def flag_arrival(d):
        at = lax.rem(z + RING - d, RING)
        return send(flags_v.at[at], flags_v.at[at], fz_s.at[d - 1], fz_r.at[d - 1], z_peer(d))

    for copy in flag_copies:
        copy.start()

    def ring_right(ref, k, s, r, to, me):
        at = lax.rem(me + RING - k, RING)
        return send(ref(at), ref(at), s.at[k], r.at[k], to)

    def ring_left(ref, k, s, r, to, me):
        at = lax.rem(me + k, RING)
        return send(ref(at), ref(at), s.at[k], r.at[k], to)

    def tok_at(at):
        return tok_all.at[at, c]

    def tok_right(k):
        return ring_right(tok_at, k, tr_s, tr_r, y_up, y)

    def tok_left(k):
        return ring_left(tok_at, k, tl_s, tl_r, y_down, y)

    def tok_sib(k, at):
        return send(tok_all.at[at, c], tok_all.at[at, c], ts_s.at[k], ts_r.at[k], sibling)

    def right_recv(ref, k, s, r, to, me):
        at = lax.rem(me + RING - k - 1, RING)
        send(ref(at), ref(at), s.at[k], r.at[k], to).wait_recv()

    def left_recv(ref, k, s, r, to, me):
        at = lax.rem(me + k + 1, RING)
        send(ref(at), ref(at), s.at[k], r.at[k], to).wait_recv()

    def tok_place(offset):
        return lax.rem(y + offset + RING, RING)

    order = [0, -1, 1, -2, 2, -3, 3, -4]
    tok_right(0).start()
    tok_left(0).start()
    tok_sib(0, y).start()

    def tok_step(k):
        right_recv(tok_at, k, tr_s, tr_r, y_up, y)
        if k < 3:
            tok_right(k + 1).start()
        tok_sib(2 * k + 1, tok_place(-k - 1)).start()
        if k < 3:
            left_recv(tok_at, k, tl_s, tl_r, y_down, y)
            if k < 2:
                tok_left(k + 1).start()
            tok_sib(2 * k + 2, tok_place(k + 1)).start()

    for d in range(1, RING):
        flag_arrival(d).wait_recv()
    for d in range(XS):
        stage_v[d] = flags_v[:, lax.rem(x + d, XS)]
    table_copies = [
        send(stage_v.at[d], table_v.at[d], fx_s.at[d - 1], fx_r.at[d - 1], x_peer(d)) for d in range(1, XS)
    ]
    for copy in table_copies:
        copy.start()
    table_v[0] = stage_v[0]
    flags_to_s = pltpu.make_async_copy(flags_v, flags_s, sm_sem.at[0])
    flags_to_s.start()
    for copy in table_copies:
        copy.wait_recv()
    table_to_s = pltpu.make_async_copy(table_v, table_s, sm_sem.at[1])
    table_to_s.start()
    loads[0].wait()
    table_to_s.wait()
    tok_step(0)

    def kv_copy(d, i):
        return send(kv_send.at[d - 1, i], kv_all.at[d, i], kv_s.at[d - 1, i], kv_r.at[d - 1, i], x_peer(d))

    def pack(i, carry):
        zr = lax.rem(z + ring_offset(i) + RING, RING)
        for d in (2, 1, 3, 0):
            for slot in range(2):
                block = table_s[(XS - d) % XS, zr, 0, slot]
                key = mem_v[0, block]
                value = mem_v[1, block].astype(F32).T.astype(BF16)
                if d:
                    kv_send[d - 1, i, slot] = key
                    kv_send[d - 1, i, 2 + slot] = value
                else:
                    kv_all[0, i, slot] = key
                    kv_all[0, i, 2 + slot] = value
            if d:
                kv_copy(d, i).start()
        return carry

    lax.fori_loop(0, 4, pack, 0)
    tok_step(1)
    lax.fori_loop(4, 8, pack, 0)
    tok_step(2)
    tok_step(3)
    flags_to_s.wait()
    loads[1].wait()

    for k in range(RING):
        at = tok_place(order[k])
        theirs = tok_all.at[at, 1 - c]
        send(theirs, theirs, ts_s.at[k], ts_r.at[k], sibling).wait_recv()
        a = tok_all[at, 0].astype(F32)
        b = tok_all[at, 1].astype(F32)
        left = jnp.concatenate([a[:rows], b[:rows]], axis=0)
        right = jnp.concatenate([a[rows:], b[rows:]], axis=0)
        x_all[pl.ds(pl.multiple_of(at * 2 * rows, 16), 2 * rows), :] = jnp.concatenate(
            [left, right], axis=1
        ).astype(BF16)

    projected = jnp.dot(x_all[...], wi_v[...], preferred_element_type=F32)
    q_all[z] = projected[:, :HD].T.astype(BF16)
    keys_v[...] = projected[:, HD : 2 * HD].astype(BF16)
    vals_v[...] = projected[:, 2 * HD :].T.astype(BF16)

    def q_at(at):
        return q_all.at[at]

    def q_right(k):
        return ring_right(q_at, k, qr_s, qr_r, z_up, z)

    def q_left(k):
        return ring_left(q_at, k, ql_s, ql_r, z_down, z)

    def q_step(k):
        right_recv(q_at, k, qr_s, qr_r, z_up, z)
        if k < 3:
            q_right(k + 1).start()
            left_recv(q_at, k, ql_s, ql_r, z_down, z)
            if k < 2:
                q_left(k + 1).start()

    q_right(0).start()
    q_left(0).start()
    blocks = keys_v.shape[0] // BLK
    last = (blocks - 1) * BLK
    halo_copies = [
        send(keys_v.at[pl.ds(last, BLK)], halo.at[0], h_s.at[0], h_r.at[0], following),
        send(vals_v.at[:, pl.ds(last, BLK)], halo.at[1], h_s.at[1], h_r.at[1], following),
    ]
    for copy in halo_copies:
        copy.start()

    unit = HD ** (-0.5) * 1.4426950408889634

    key_row = lax.broadcasted_iota(jnp.int32, (BLK, BLK), 0)
    query_col = lax.broadcasted_iota(jnp.int32, (BLK, BLK), 1)

    def near(j):
        cols = slice(j * BLK, (j + 1) * BLK)
        query = q_all[z, :, cols]
        if j == 0:
            key0, val0 = halo[0], halo[1]
            seen = jnp.where(m > 0, 0.0, NONE).astype(F32)
        else:
            key0 = keys_v[(j - 1) * BLK : j * BLK, :]
            val0 = vals_v[:, (j - 1) * BLK : j * BLK]
            seen = None
        s0 = jnp.dot(key0, query, preferred_element_type=F32) * unit
        s1 = jnp.dot(keys_v[cols, :], query, preferred_element_type=F32) * unit
        s0 = jnp.where(key_row > query_col, s0, NONE)
        s1 = jnp.where(key_row <= query_col, s1, NONE)
        if seen is not None:
            s0 = s0 + seen
        peak = jnp.maximum(jnp.max(s0, axis=0, keepdims=True), jnp.max(s1, axis=0, keepdims=True))
        p0 = jnp.exp2(s0 - peak)
        p1 = jnp.exp2(s1 - peak)
        total = jnp.sum(p0, axis=0, keepdims=True) + jnp.sum(p1, axis=0, keepdims=True)
        o = jnp.dot(val0, p0.astype(BF16), preferred_element_type=F32)
        o = o + jnp.dot(vals_v[:, cols], p1.astype(BF16), preferred_element_type=F32)
        near_v[:, cols] = o * (1.0 / total)

    q_step(0)
    near(1)
    q_step(1)
    near(2)
    q_step(2)
    for copy in halo_copies:
        copy.wait_recv()
    near(0)
    q_step(3)

    def o_copies(i, to):
        return (
            send(o_send.at[i], o_recv.at[i], o_s.at[i], o_r.at[i], to),
            send(l_send.at[i], l_recv.at[i], l_s.at[i], l_r.at[i], to),
        )

    def merge(i):
        for copy in o_copies(i, z_up):
            copy.wait_recv()
        la, lb = lse_v[0:1, :], l_recv[i][0:1, :]
        top = jnp.maximum(la, lb)
        wa, wb = jnp.exp2(la - top), jnp.exp2(lb - top)
        total = wa + wb
        inverse = 1.0 / total
        far_v[...] = (wa * inverse) * far_v[...] + (wb * inverse) * o_recv[i].astype(F32)
        lse_v[...] = jnp.broadcast_to(top + jnp.log2(total), lse_v.shape)

    def attend(i, carry):
        zr = lax.rem(z + ring_offset(i) + RING, RING)
        for d in range(1, XS):
            kv_copy(d, i).wait_recv()
        for j in range(blocks):
            cols = slice(j * BLK, (j + 1) * BLK)
            query = q_all[zr, :, cols]
            scores = []
            peak = None
            for d in range(XS):
                holder = lax.rem(x + XS - d, XS)
                keys = kv_all[d, i, 0:2].reshape(2 * BLK, HD)
                s = jnp.dot(keys, query, preferred_element_type=F32) * unit
                for slot in range(2):
                    flag = flags_s[zr, holder, 0, 2 + 2 * j + slot].astype(F32)
                    one = s[slot * BLK : (slot + 1) * BLK] + (flag - 1.0) * (-NONE)
                    scores.append(one)
                    high = jnp.max(one, axis=0, keepdims=True)
                    peak = high if peak is None else jnp.maximum(peak, high)
            total = None
            o = None
            for d in range(XS):
                p = [jnp.exp2(scores[2 * d + slot] - peak) for slot in range(2)]
                count = jnp.sum(p[0] + p[1], axis=0, keepdims=True)
                total = count if total is None else total + count
                probs = jnp.concatenate([p[0].astype(BF16), p[1].astype(BF16)], axis=0)
                vals = jnp.concatenate([kv_all[d, i, 2], kv_all[d, i, 3]], axis=1)
                term = jnp.dot(vals, probs, preferred_element_type=F32)
                o = term if o is None else o + term
            far_v[:, cols] = o * (1.0 / total)
            lse_v[:, cols] = jnp.broadcast_to(peak + jnp.log2(total), (8, BLK))

        @pl.when(i >= 2)
        def _():
            merge(i - 2)

        @pl.when(i < 7)
        def _():
            up = lax.rem(i, 2) == 0
            to = (jnp.where(up, z_up[0], z_down[0]), t)
            o_send[i] = far_v[...].astype(BF16)
            l_send[i] = lse_v[...]
            for copy in o_copies(i, to):
                copy.start()

        return carry

    lax.fori_loop(0, 8, attend, 0)
    merge(6)

    share = 1.0 / (1.0 + jnp.exp(jnp.full((1, HD), -gate_ref[0], F32)))
    share = share[:, 0:1]
    attended = (share * far_v[...] + (1.0 - share) * near_v[...]).T.astype(BF16)
    loads[2].wait()
    width = 256

    def project_out(n, carry):
        at_left = pl.multiple_of(n * width, width)
        at_right = pl.multiple_of(half + n * width, width)
        left = jnp.dot(attended, wo_v[:, pl.ds(at_left, width)], preferred_element_type=F32)
        right = jnp.dot(attended, wo_v[:, pl.ds(at_right, width)], preferred_element_type=F32)
        for k in range(2 * RING):
            part[k, :, pl.ds(at_left, width)] = jnp.concatenate(
                [left[k * rows : (k + 1) * rows], right[k * rows : (k + 1) * rows]], axis=0
            ).astype(BF16)
        return carry

    lax.fori_loop(0, half // width, project_out, 0)

    def y_place(i):
        return lax.rem(y + ring_offset(i) + RING, RING)

    def part_copy(i):
        return send(part.at[2 * y_place(i) + 1 - c], sib_part.at[i], ps_s.at[i], ps_r.at[i], sibling)

    for i in range(RING):
        part_copy(i).start()

    def y_copy(i):
        return send(y_send.at[i], y_recv.at[i], y_s.at[i], y_r.at[i], y_up if i % 2 == 0 else y_down)

    for i in range(RING):
        part_copy(i).wait_recv()
        total = part[2 * y_place(i) + c].astype(F32) + sib_part[i].astype(F32)
        if i >= 2:
            y_copy(i - 2).wait_recv()
            total = total + y_recv[i - 2].astype(F32)
        if i < 7:
            y_send[i] = total.astype(BF16)
            y_copy(i).start()
        else:
            y_copy(6).wait_recv()
            total = total + y_recv[6].astype(F32)
            out_ref[...] = jnp.concatenate([total[:rows], total[rows:]], axis=1).astype(BF16)

    for copy in flag_copies + table_copies + halo_copies:
        copy.wait_send()
    for k in range(4):
        tok_right(k).wait_send()
        q_right(k).wait_send()
    for k in range(3):
        tok_left(k).wait_send()
        q_left(k).wait_send()
    for k in range(RING):
        tok_sib(k, tok_place(order[k])).wait_send()
        part_copy(k).wait_send()
    for i in range(7):
        for copy in o_copies(i, z_up):
            copy.wait_send()
        y_copy(i).wait_send()

    def kv_sent(i, carry):
        for d in range(1, XS):
            kv_copy(d, i).wait_send()
        return carry

    lax.fori_loop(0, 8, kv_sent, 0)


def requests(retrieved, block_home, owners, blocks_per_owner):
    rows, entries = retrieved.shape
    every = jnp.arange(block_home.shape[0], dtype=jnp.int32)
    home = jnp.sum(jnp.where(retrieved[:, :, None] == every, block_home[None, None, :], 0), axis=-1)
    named = jnp.any(home[:, :, None] == every, axis=1).reshape(rows, owners, blocks_per_owner)
    local_id = jnp.arange(blocks_per_owner, dtype=jnp.int32)
    anyone = jnp.any(named, axis=0)
    first = jnp.min(jnp.where(anyone, local_id, blocks_per_owner - 1), axis=-1)
    second = jnp.max(jnp.where(anyone, local_id, 0), axis=-1)
    of_first = jnp.any(named & (local_id == first[:, None]), axis=-1)
    of_second = jnp.any(named & (local_id == second[:, None]), axis=-1) & (second != first)
    flags = jnp.stack([of_first, of_second], axis=-1).astype(jnp.int32)
    flags = jnp.transpose(flags, (1, 0, 2)).reshape(owners, 2 * rows)
    record = jnp.concatenate([first[:, None], second[:, None], flags], axis=1)
    record = jnp.pad(record, ((0, 0), (0, 128 - record.shape[1])))
    return record.reshape(RING, XS, 1, 128)


def local(tokens, input_weight, output_weight, gate_logit, memory, retrieved, block_home):
    rows, width = tokens.shape
    store = memory.reshape(2, memory.shape[1] // BLK, BLK, HD)
    span = rows * 2 * RING
    record = requests(retrieved, block_home, RING * XS, memory.shape[1] // BLK)
    vmem = pltpu.VMEM
    dma = pltpu.SemaphoreType.DMA
    packed = (2 * rows, width // 2)
    scratch = [
        vmem((RING, 2) + packed, BF16),
        vmem((span, width), BF16),
        vmem(input_weight.shape, BF16),
        vmem(output_weight.shape, BF16),
        vmem(store.shape, BF16),
        vmem((RING, XS, 1, 128), jnp.int32),
        vmem((XS, RING, 1, 128), jnp.int32),
        vmem((XS, RING, 1, 128), jnp.int32),
        pltpu.SMEM((RING, XS, 1, 128), jnp.int32),
        pltpu.SMEM((XS, RING, 1, 128), jnp.int32),
        vmem((XS - 1, RING, 4, BLK, HD), BF16),
        vmem((XS, RING, 4, BLK, HD), BF16),
        vmem((RING, HD, span), BF16),
        vmem((span, HD), BF16),
        vmem((HD, span), BF16),
        vmem((2, BLK, HD), BF16),
        vmem((HD, span), F32),
        vmem((HD, span), F32),
        vmem((8, span), F32),
        vmem((7, HD, span), BF16),
        vmem((7, HD, span), BF16),
        vmem((7, 8, span), F32),
        vmem((7, 8, span), F32),
        vmem((2 * RING,) + packed, BF16),
        vmem((RING,) + packed, BF16),
        vmem((7,) + packed, BF16),
        vmem((7,) + packed, BF16),
        dma((3,)),
        dma((4,)), dma((4,)), dma((3,)), dma((3,)), dma((8,)), dma((8,)),
        dma((7,)), dma((7,)), dma((3,)), dma((3,)), dma((2,)),
        dma((3, 8)), dma((3, 8)), dma((4,)), dma((4,)), dma((3,)), dma((3,)), dma((2,)), dma((2,)),
        dma((7,)), dma((7,)), dma((7,)), dma((7,)), dma((8,)), dma((8,)), dma((7,)), dma((7,)),
    ]
    whole = pl.BlockSpec(memory_space=pltpu.VMEM)
    outside = pl.BlockSpec(memory_space=pl.ANY)
    return pl.pallas_call(
        kernel,
        out_shape=jax.ShapeDtypeStruct(tokens.shape, BF16),
        in_specs=[whole, whole, pl.BlockSpec(memory_space=pltpu.SMEM), outside, outside, outside],
        out_specs=whole,
        scratch_shapes=scratch,
        compiler_params=pltpu.CompilerParams(
            collective_id=0, has_side_effects=True, vmem_limit_bytes=56 * 2**20
        ),
    )(tokens, record, gate_logit, input_weight, output_weight, store)


def solution(mesh):
    placed = (
        P(("mem", "tp"), None),
        P(None, "tp"),
        P("tp", None),
        P("tp"),
        P(None, "mem", "tp"),
        P("mem", None),
        P(),
    )
    return jax.shard_map(
        local, mesh=mesh, in_specs=placed, out_specs=P(("mem", "tp"), None), check_vma=False
    )
```

```python
import functools

import jax
import jax.numpy as jnp
from jax import lax
from jax.experimental import pallas as pl
from jax.experimental.pallas import tpu as pltpu
from jax.sharding import PartitionSpec as P

HD = 128
BLK = 128
XS = 4
RING = 8
MESH = pl.DeviceIdType.MESH
NONE = -1e30
BF16 = jnp.bfloat16
F32 = jnp.float32


def ring_offset(step):
    half = step // 2
    even = lax.rem(step, 2) == 0 if not isinstance(step, int) else step % 2 == 0
    if isinstance(step, int):
        return (4 - half) if even else (half - 3)
    return jnp.where(even, 4 - half, half - 3)


def kernel(
    ret_ref, home_ref, gate_ref, tok_ref, wi_hbm, wo_hbm, mem_hbm, out_ref,
    tok_all, x_all, wi_v, wo_all, mem_v,
    rec_v, table_v, table_s,
    kv_send, kv_all, q_all, keys_v, vals_v, halo,
    near_v, far_v, lse_v, o_send, o_recv, l_send, l_recv,
    att_v, att_send, att_all, part, y_send, y_recv,
    in_sem,
    tr_s, tr_r, tl_s, tl_r, ts_s, ts_r, rec_s, rec_r,
    kv_s, kv_r, qr_s, qr_r, ql_s, ql_r, h_s, h_r,
    o_s, o_r, l_s, l_r, w_s, w_r, a_s, a_r, y_s, y_r,
):
    m = lax.axis_index("mem")
    t = lax.axis_index("tp")
    z, x = m // XS, lax.rem(m, XS)
    y, c = t // 2, lax.rem(t, 2)
    nmem = RING * XS

    def at_y(where, core):
        return (m, lax.rem(where + RING, RING) * 2 + core)

    sibling = at_y(y, 1 - c)
    y_up, y_down = at_y(y + 1, c), at_y(y - 1, c)
    across, across_other = at_y(y + 4, c), at_y(y + 4, 1 - c)
    z_up = (lax.rem(z + 1, RING) * XS + x, t)
    z_down = (lax.rem(z + RING - 1, RING) * XS + x, t)
    following = (lax.rem(m + 1, nmem), t)

    def mem_peer(d):
        return (lax.rem(m + d, nmem), t)

    def x_peer(d):
        return (z * XS + lax.rem(x + d, XS), t)

    def send(src, dst, s, r, to):
        return pltpu.make_async_remote_copy(
            src_ref=src, dst_ref=dst, send_sem=s, recv_sem=r, device_id=to, device_id_type=MESH
        )

    loads = [
        pltpu.make_async_copy(mem_hbm, mem_v, in_sem.at[0]),
        pltpu.make_async_copy(wi_hbm, wi_v, in_sem.at[1]),
        pltpu.make_async_copy(wo_hbm, wo_all.at[0], in_sem.at[2]),
    ]

    barrier = pltpu.get_barrier_semaphore()
    partners = [sibling, y_up, y_down, across, across_other]
    for to in partners:
        pl.semaphore_signal(barrier, inc=1, device_id=to, device_id_type=MESH)

    def greet(d, carry):
        pl.semaphore_signal(barrier, inc=1, device_id=mem_peer(d), device_id_type=MESH)
        return carry

    lax.fori_loop(1, nmem, greet, 0)
    for load in loads:
        load.start()

    own = tok_ref[...].astype(F32)
    half = own.shape[1] // 2
    rows = own.shape[0]
    tok_all[y, c] = jnp.concatenate([own[:, :half], own[:, half:]], axis=0).astype(BF16)

    lane = lax.broadcasted_iota(jnp.int32, (RING, 128), 1)
    place = lax.broadcasted_iota(jnp.int32, (RING, 128), 0) * 128 + lane
    number = lax.rem(lane, 32)
    names = jnp.zeros((RING, 128), jnp.int32)
    blocks, entries = ret_ref.shape
    for j in range(blocks):
        hit = jnp.zeros((RING, 128), jnp.int32)
        for e in range(entries):
            hit = jnp.where(place == home_ref[ret_ref[j, e]], 1, hit)
        names = names + hit * (1 << j)
    word = number * 8 + names
    low = jnp.where(names > 0, word, 31 * 8)
    high = jnp.where(names > 0, word, 0)
    for k in (1, 2, 4, 8, 16):
        inside = number + k < 32
        low = jnp.where(inside, jnp.minimum(low, pltpu.roll(low, 128 - k, 1)), low)
        high = jnp.where(inside, jnp.maximum(high, pltpu.roll(high, 128 - k, 1)), high)
    high = jnp.where(high == low, high - (high & 7), high)
    record = jnp.where(number == 0, low, pltpu.roll(high, 1, 1))
    for k in range(RING):
        rec_v[k] = record[k : k + 1]
    table_v[m] = rec_v[z]

    pl.semaphore_wait(barrier, len(partners) + nmem - 1)

    def ring_right(ref, k, s, r, to, me):
        at = lax.rem(me + RING - k, RING)
        return send(ref(at), ref(at), s.at[k], r.at[k], to)

    def ring_left(ref, k, s, r, to, me):
        at = lax.rem(me + k, RING)
        return send(ref(at), ref(at), s.at[k], r.at[k], to)

    def tok_at(at):
        return tok_all.at[at, c]

    def tok_right(k):
        return ring_right(tok_at, k, tr_s, tr_r, y_up, y)

    def tok_left(k):
        return ring_left(tok_at, k, tl_s, tl_r, y_down, y)

    def tok_sib(k, at):
        return send(tok_all.at[at, c], tok_all.at[at, c], ts_s.at[k], ts_r.at[k], sibling)

    def right_recv(ref, k, s, r, to, me):
        at = lax.rem(me + RING - k - 1, RING)
        send(ref(at), ref(at), s.at[k], r.at[k], to).wait_recv()

    def left_recv(ref, k, s, r, to, me):
        at = lax.rem(me + k + 1, RING)
        send(ref(at), ref(at), s.at[k], r.at[k], to).wait_recv()

    def tok_place(offset):
        return lax.rem(y + offset + RING, RING)

    order = [0, -1, 1, -2, 2, -3, 3, -4]
    tok_right(0).start()
    tok_left(0).start()
    tok_sib(0, y).start()

    def tok_step(k):
        right_recv(tok_at, k, tr_s, tr_r, y_up, y)
        if k < 3:
            tok_right(k + 1).start()
        tok_sib(2 * k + 1, tok_place(-k - 1)).start()
        if k < 3:
            left_recv(tok_at, k, tl_s, tl_r, y_down, y)
            if k < 2:
                tok_left(k + 1).start()
            tok_sib(2 * k + 2, tok_place(k + 1)).start()

    def rec_copy(d):
        return send(
            rec_v.at[lax.rem(m + d, nmem) // XS], table_v.at[m], rec_s.at[d - 1], rec_r.at[d - 1], mem_peer(d)
        )

    def rec_start(d, carry):
        rec_copy(d).start()
        return carry

    def rec_wait(d, carry):
        at = table_v.at[lax.rem(m + nmem - d, nmem)]
        send(at, at, rec_s.at[d - 1], rec_r.at[d - 1], mem_peer(d)).wait_recv()
        return carry

    lax.fori_loop(1, nmem, rec_start, 0)
    lax.fori_loop(1, nmem, rec_wait, 0)
    table_to_s = pltpu.make_async_copy(table_v, table_s, in_sem.at[3])
    table_to_s.start()
    tok_step(0)
    loads[0].wait()
    table_to_s.wait()

    def kv_copy(d, i):
        return send(kv_send.at[d - 1, i], kv_all.at[d, i], kv_s.at[d - 1, i], kv_r.at[d - 1, i], x_peer(d))

    def pack(i, carry):
        zr = lax.rem(z + ring_offset(i) + RING, RING)
        for d in (2, 1, 3, 0):
            for slot in range(2):
                words = table_s[zr * XS + lax.rem(x + d, XS), 0, x * 32 + slot]
                block = lax.shift_right_logical(words, 3)
                key = mem_v[0, block]
                value = mem_v[1, block].astype(F32).T.astype(BF16)
                if d:
                    kv_send[d - 1, i, slot] = key
                    kv_send[d - 1, i, 2 + slot] = value
                else:
                    kv_all[0, i, slot] = key
                    kv_all[0, i, 2 + slot] = value
            if d:
                kv_copy(d, i).start()
        return carry

    lax.fori_loop(0, 4, pack, 0)
    tok_step(1)
    lax.fori_loop(4, 8, pack, 0)
    tok_step(2)
    tok_step(3)
    loads[1].wait()
    loads[2].wait()

    weight_copies = [
        send(wo_all.at[0], wo_all.at[1], w_s.at[0], w_r.at[0], sibling),
        send(wo_all.at[0], wo_all.at[2], w_s.at[1], w_r.at[1], across),
        send(wo_all.at[2], wo_all.at[3], w_s.at[2], w_r.at[2], sibling),
    ]

    for k in range(RING):
        at = tok_place(order[k])
        theirs = tok_all.at[at, 1 - c]
        send(theirs, theirs, ts_s.at[k], ts_r.at[k], sibling).wait_recv()
        a = tok_all[at, 0].astype(F32)
        b = tok_all[at, 1].astype(F32)
        left = jnp.concatenate([a[:rows], b[:rows]], axis=0)
        right = jnp.concatenate([a[rows:], b[rows:]], axis=0)
        x_all[pl.ds(pl.multiple_of(at * 2 * rows, 16), 2 * rows), :] = jnp.concatenate(
            [left, right], axis=1
        ).astype(BF16)

    projected = jnp.dot(x_all[...], wi_v[...], preferred_element_type=F32)
    q_all[z] = projected[:, :HD].T.astype(BF16)
    keys_v[...] = projected[:, HD : 2 * HD].astype(BF16)
    vals_v[...] = projected[:, 2 * HD :].T.astype(BF16)

    def q_at(at):
        return q_all.at[at]

    def q_right(k):
        return ring_right(q_at, k, qr_s, qr_r, z_up, z)

    def q_left(k):
        return ring_left(q_at, k, ql_s, ql_r, z_down, z)

    def q_step(k):
        right_recv(q_at, k, qr_s, qr_r, z_up, z)
        if k < 3:
            q_right(k + 1).start()
            left_recv(q_at, k, ql_s, ql_r, z_down, z)
            if k < 2:
                q_left(k + 1).start()

    q_right(0).start()
    q_left(0).start()
    last = (blocks - 1) * BLK
    halo_copies = [
        send(keys_v.at[pl.ds(last, BLK)], halo.at[0], h_s.at[0], h_r.at[0], following),
        send(vals_v.at[:, pl.ds(last, BLK)], halo.at[1], h_s.at[1], h_r.at[1], following),
    ]
    for copy in halo_copies:
        copy.start()
    weight_copies[1].start()
    weight_copies[0].start()

    unit = HD ** (-0.5) * 1.4426950408889634

    key_row = lax.broadcasted_iota(jnp.int32, (BLK, BLK), 0)
    query_col = lax.broadcasted_iota(jnp.int32, (BLK, BLK), 1)

    def near(j):
        cols = slice(j * BLK, (j + 1) * BLK)
        query = q_all[z, :, cols]
        if j == 0:
            key0, val0 = halo[0], halo[1]
            seen = jnp.where(m > 0, 0.0, NONE).astype(F32)
        else:
            key0 = keys_v[(j - 1) * BLK : j * BLK, :]
            val0 = vals_v[:, (j - 1) * BLK : j * BLK]
            seen = None
        s0 = jnp.dot(key0, query, preferred_element_type=F32) * unit
        s1 = jnp.dot(keys_v[cols, :], query, preferred_element_type=F32) * unit
        s0 = jnp.where(key_row > query_col, s0, NONE)
        s1 = jnp.where(key_row <= query_col, s1, NONE)
        if seen is not None:
            s0 = s0 + seen
        peak = jnp.maximum(jnp.max(s0, axis=0, keepdims=True), jnp.max(s1, axis=0, keepdims=True))
        p0 = jnp.exp2(s0 - peak)
        p1 = jnp.exp2(s1 - peak)
        total = jnp.sum(p0, axis=0, keepdims=True) + jnp.sum(p1, axis=0, keepdims=True)
        o = jnp.dot(val0, p0.astype(BF16), preferred_element_type=F32)
        o = o + jnp.dot(vals_v[:, cols], p1.astype(BF16), preferred_element_type=F32)
        near_v[:, cols] = o * (1.0 / total)

    q_step(0)
    near(1)
    q_step(1)
    near(2)
    q_step(2)
    for copy in halo_copies:
        copy.wait_recv()
    near(0)
    q_step(3)

    def o_copies(i, to):
        return (
            send(o_send.at[i], o_recv.at[i], o_s.at[i], o_r.at[i], to),
            send(l_send.at[i], l_recv.at[i], l_s.at[i], l_r.at[i], to),
        )

    def merge(i):
        for copy in o_copies(i, z_up):
            copy.wait_recv()
        la, lb = lse_v[0:1, :], l_recv[i][0:1, :]
        top = jnp.maximum(la, lb)
        wa, wb = jnp.exp2(la - top), jnp.exp2(lb - top)
        total = wa + wb
        inverse = 1.0 / total
        far_v[...] = (wa * inverse) * far_v[...] + (wb * inverse) * o_recv[i].astype(F32)
        lse_v[...] = jnp.broadcast_to(top + jnp.log2(total), lse_v.shape)

    def attend(i, carry):
        zr = lax.rem(z + ring_offset(i) + RING, RING)
        for d in range(1, XS):
            kv_copy(d, i).wait_recv()
        for j in range(blocks):
            cols = slice(j * BLK, (j + 1) * BLK)
            query = q_all[zr, :, cols]
            scores = []
            peak = None
            for d in range(XS):
                holder = lax.rem(x + XS - d, XS)
                keys = kv_all[d, i, 0:2].reshape(2 * BLK, HD)
                s = jnp.dot(keys, query, preferred_element_type=F32) * unit
                for slot in range(2):
                    words = table_s[zr * XS + x, 0, holder * 32 + slot]
                    flag = (lax.shift_right_logical(words, j) & 1).astype(F32)
                    one = s[slot * BLK : (slot + 1) * BLK] + (flag - 1.0) * (-NONE)
                    scores.append(one)
                    high = jnp.max(one, axis=0, keepdims=True)
                    peak = high if peak is None else jnp.maximum(peak, high)
            total = None
            o = None
            for d in range(XS):
                p = [jnp.exp2(scores[2 * d + slot] - peak) for slot in range(2)]
                count = jnp.sum(p[0] + p[1], axis=0, keepdims=True)
                total = count if total is None else total + count
                probs = jnp.concatenate([p[0].astype(BF16), p[1].astype(BF16)], axis=0)
                vals = jnp.concatenate([kv_all[d, i, 2], kv_all[d, i, 3]], axis=1)
                term = jnp.dot(vals, probs, preferred_element_type=F32)
                o = term if o is None else o + term
            far_v[:, cols] = o * (1.0 / total)
            lse_v[:, cols] = jnp.broadcast_to(peak + jnp.log2(total), (8, BLK))

        @pl.when(i >= 2)
        def _():
            merge(i - 2)

        @pl.when(i < 7)
        def _():
            up = lax.rem(i, 2) == 0
            to = (jnp.where(up, z_up[0], z_down[0]), t)
            o_send[i] = far_v[...].astype(BF16)
            l_send[i] = lse_v[...]
            for copy in o_copies(i, to):
                copy.start()

        return carry

    lax.fori_loop(0, 6, attend, 0)
    weight_copies[1].wait_recv()
    weight_copies[2].start()
    lax.fori_loop(6, 8, attend, 0)
    merge(6)

    share = 1.0 / (1.0 + jnp.exp(jnp.full((1, HD), -gate_ref[0], F32)))
    share = share[:, 0:1]
    att_v[...] = (share * far_v[...] + (1.0 - share) * near_v[...]).T

    def rows_for(where, core):
        ahead = 1 - 2 * core
        picked = []
        for o in (2, 1, 0, -1):
            chip = lax.rem(where + o * ahead + 2 * RING, RING)
            picked.append(att_v[pl.ds(pl.multiple_of((chip * 2 + core) * rows, 8), rows), :])
        return jnp.concatenate(picked, axis=0).astype(BF16)

    att_copies = [
        send(att_send.at[0], att_all.at[2], a_s.at[0], a_r.at[0], across),
        send(att_send.at[1], att_all.at[3], a_s.at[1], a_r.at[1], across_other),
        send(att_send.at[2], att_all.at[1], a_s.at[2], a_r.at[2], sibling),
    ]
    for k, (where, core) in enumerate(((y + 4, c), (y + 4, 1 - c), (y, 1 - c))):
        att_send[k] = rows_for(where, core)
        att_copies[k].start()
    att_all[0] = rows_for(y, c)
    weight_copies[0].wait_recv()
    weight_copies[2].wait_recv()
    for copy in att_copies:
        copy.wait_recv()
    attended = jnp.concatenate([att_all[k] for k in range(4)], axis=1)
    width = 256

    def project_out(n, carry):
        at_left = pl.multiple_of(n * width, width)
        at_right = pl.multiple_of(half + n * width, width)

        def columns(at):
            weights = jnp.concatenate([wo_all[k, :, pl.ds(at, width)] for k in range(4)], axis=0)
            return jnp.dot(attended, weights, preferred_element_type=F32)

        left, right = columns(at_left), columns(at_right)
        for k in range(4):
            part[k, :, pl.ds(at_left, width)] = jnp.concatenate(
                [left[k * rows : (k + 1) * rows], right[k * rows : (k + 1) * rows]], axis=0
            )
        return carry

    lax.fori_loop(0, half // width, project_out, 0)

    ahead, behind = at_y(y + 1 - 2 * c, c), at_y(y - 1 + 2 * c, c)
    y_copies = [
        send(y_send.at[k], y_recv.at[k], y_s.at[k], y_r.at[k], behind if k == 2 else ahead) for k in range(3)
    ]
    y_send[0] = part[0].astype(BF16)
    y_copies[0].start()
    y_send[2] = part[3].astype(BF16)
    y_copies[2].start()

    for copy in weight_copies + halo_copies + att_copies:
        copy.wait_send()
    for k in range(4):
        tok_right(k).wait_send()
        q_right(k).wait_send()
    for k in range(3):
        tok_left(k).wait_send()
        q_left(k).wait_send()
    for k in range(RING):
        tok_sib(k, tok_place(order[k])).wait_send()
    for i in range(7):
        for copy in o_copies(i, z_up):
            copy.wait_send()

    def rec_sent(d, carry):
        rec_copy(d).wait_send()
        return carry

    def kv_sent(i, carry):
        for d in range(1, XS):
            kv_copy(d, i).wait_send()
        return carry

    lax.fori_loop(1, nmem, rec_sent, 0)
    lax.fori_loop(0, 8, kv_sent, 0)

    y_copies[0].wait_recv()
    y_send[1] = (part[1] + y_recv[0].astype(F32)).astype(BF16)
    y_copies[1].start()
    y_copies[2].wait_recv()
    total = part[2] + y_recv[2].astype(F32)
    y_copies[1].wait_recv()
    total = total + y_recv[1].astype(F32)
    out_ref[...] = jnp.concatenate([total[:rows], total[rows:]], axis=1).astype(BF16)
    for copy in y_copies:
        copy.wait_send()


def local(tokens, input_weight, output_weight, gate_logit, memory, retrieved, block_home):
    rows, width = tokens.shape
    store = memory.reshape(2, memory.shape[1] // BLK, BLK, HD)
    span = rows * 2 * RING
    vmem = pltpu.VMEM
    dma = pltpu.SemaphoreType.DMA
    packed = (2 * rows, width // 2)
    scratch = [
        vmem((RING, 2) + packed, BF16),
        vmem((span, width), BF16),
        vmem(input_weight.shape, BF16),
        vmem((4,) + output_weight.shape, BF16),
        vmem(store.shape, BF16),
        vmem((RING, 1, 128), jnp.int32),
        vmem((RING * XS, 1, 128), jnp.int32),
        pltpu.SMEM((RING * XS, 1, 128), jnp.int32),
        vmem((XS - 1, RING, 4, BLK, HD), BF16),
        vmem((XS, RING, 4, BLK, HD), BF16),
        vmem((RING, HD, span), BF16),
        vmem((span, HD), BF16),
        vmem((HD, span), BF16),
        vmem((2, BLK, HD), BF16),
        vmem((HD, span), F32),
        vmem((HD, span), F32),
        vmem((8, span), F32),
        vmem((7, HD, span), BF16),
        vmem((7, HD, span), BF16),
        vmem((7, 8, span), F32),
        vmem((7, 8, span), F32),
        vmem((span, HD), F32),
        vmem((3, 4 * rows, HD), BF16),
        vmem((4, 4 * rows, HD), BF16),
        vmem((4,) + packed, F32),
        vmem((3,) + packed, BF16),
        vmem((3,) + packed, BF16),
        dma((4,)),
        dma((4,)), dma((4,)), dma((3,)), dma((3,)), dma((8,)), dma((8,)), dma((31,)), dma((31,)),
        dma((3, 8)), dma((3, 8)), dma((4,)), dma((4,)), dma((3,)), dma((3,)), dma((2,)), dma((2,)),
        dma((7,)), dma((7,)), dma((7,)), dma((7,)),
        dma((3,)), dma((3,)), dma((3,)), dma((3,)), dma((3,)), dma((3,)),
    ]
    whole = pl.BlockSpec(memory_space=pltpu.VMEM)
    outside = pl.BlockSpec(memory_space=pl.ANY)
    scalars = pl.BlockSpec(memory_space=pltpu.SMEM)
    return pl.pallas_call(
        kernel,
        out_shape=jax.ShapeDtypeStruct(tokens.shape, BF16),
        in_specs=[scalars, scalars, scalars, whole, outside, outside, outside],
        out_specs=whole,
        scratch_shapes=scratch,
        compiler_params=pltpu.CompilerParams(
            collective_id=0, has_side_effects=True, vmem_limit_bytes=56 * 2**20
        ),
    )(retrieved, block_home, gate_logit, tokens, input_weight, output_weight, store)


def solution(mesh):
    placed = (
        P(("mem", "tp"), None),
        P(None, "tp"),
        P("tp", None),
        P("tp"),
        P(None, "mem", "tp"),
        P("mem", None),
        P(),
    )
    return jax.shard_map(
        local, mesh=mesh, in_specs=placed, out_specs=P(("mem", "tp"), None), check_vma=False
    )
```
